512 devices in a mesh: section: 16 (over z_hi, y, core), tp: 32 (over x, z_lo).
Axes of the slice: x: 4, y: 4, z: 16 (z_hi: 2, z_lo: 8; z = z_hi * 8 + z_lo), core: 2. Of those that a mesh axis runs over, the one named last changes fastest.
Arguments:
- qkv_sent: bfloat16 [16, 768, 3, 12288], P('section', None, None, 'tp'), may hold values from -5 to 5, as said below
- grad_out: bfloat16 [16, 768, 12288], P('section', None, 'tp'), may hold values from -6 to 6
Outputs:
- attn_out: bfloat16 [16, 768, 12288], P('section', None, 'tp')
- grad_qkv: bfloat16 [16, 768, 3, 12288], P('section', None, None, 'tp')
The draws below stay inside these ranges and needn't reach their ends.
Inputs may be any that keep to these rules, and one draw needn't show every extreme that they name: `qkv_sent`: entries of the queries, keys and values are real values.
All inputs are finite; a program needn't handle non-finite values.
Results may differ from the reference program's by a relative error of at most 0.014.
Values may be sent and summed in bfloat16 or wider, within the bound.
No kernel may reach another device: no remote copies, remote signals or barrier semaphores. Data moves between devices by JAX's collectives and lax.ppermute only.
A program may use at most 64 MiB of HBM per device.

```python
import math
import jax
import jax.numpy as jnp
from jax import lax

HEADS = 96
HD = 128
LEN = 768
D = 12288
SECTIONS = 16


def draw_qkv_sent(key, part):
    keys_list = jax.random.split(jax.random.fold_in(key, 17), 1)
    shape = (SECTIONS, LEN, 3, HEADS, HD)
    field = jnp.clip(jax.random.normal(keys_list[0], shape, jnp.float32), -5.0, 5.0)
    return field.reshape(SECTIONS, LEN, 3, D).astype(jnp.bfloat16)


def levels(key, extent, cuts, least, high):
    def one(axis_at, parts):
        draws = jax.random.uniform(jax.random.fold_in(jax.random.fold_in(key, 6), axis_at), (parts,), jnp.float32, least / len(cuts), high / len(cuts))
        return jnp.repeat(jnp.exp(draws), extent[axis_at] // parts).reshape((-1,) + (1,) * (len(extent) - axis_at - 1))

    gain = one(*cuts[0])
    for cut in cuts[1:]:
        gain = gain * one(*cut)
    return gain


def centred(rng, extent, scale, bound, cuts=(), held_as=jnp.bfloat16):
    drawn = jax.random.normal(rng, extent, jnp.float32) * scale
    if len(cuts) > 0:
        drawn = levels(rng, extent, cuts, -0.22, 0.18) * drawn
    return jnp.clip(drawn, min=-bound, max=bound).astype(held_as)


def setup_inputs(seed: int = 0) -> dict:
    key_of = jax.random.split(jax.random.key(seed), 3)
    qkv_sent = draw_qkv_sent(jax.random.fold_in(key_of[2], 71), 0)
    grad_out = centred(key_of[1], (SECTIONS, LEN, D), 1.0, 6.0, ((0, 16), (2, 32)))
    return dict(qkv_sent=qkv_sent, grad_out=grad_out)


def head_pass(query, keys, values, dout):
    scale = 1.0 / math.sqrt(HD)
    hp = lax.Precision.HIGHEST
    qf = query.astype(jnp.float32)
    kf = keys.astype(jnp.float32)
    vf = values.astype(jnp.float32)
    df = dout.astype(jnp.float32)
    scores = jnp.dot(qf, kf.T, precision=hp) * scale
    rows = lax.broadcasted_iota(jnp.int32, scores.shape, 0)
    cols = lax.broadcasted_iota(jnp.int32, scores.shape, 1)
    scores = jnp.where(cols <= rows, scores, -jnp.inf)
    peak = lax.optimization_barrier(jnp.max(scores, axis=1, keepdims=True))
    expo = jnp.exp(scores - peak)
    probs = expo / lax.optimization_barrier(jnp.sum(expo, axis=1, keepdims=True))
    weights = probs.astype(jnp.bfloat16)
    wf = weights.astype(jnp.float32)
    output = jnp.dot(wf, vf, precision=hp).astype(jnp.bfloat16)
    grad_v = jnp.dot(wf.T, df, precision=hp).astype(jnp.bfloat16)
    grad_p = jnp.dot(df, vf.T, precision=hp)
    delta = lax.optimization_barrier(jnp.sum(df * output.astype(jnp.float32), axis=1, keepdims=True))
    grad_s = (probs * (grad_p - delta)).astype(jnp.bfloat16).astype(jnp.float32)
    grad_q = (jnp.dot(grad_s, kf, precision=hp) * scale).astype(jnp.bfloat16)
    grad_k = (jnp.dot(grad_s.T, qf, precision=hp) * scale).astype(jnp.bfloat16)
    return (output, grad_q, grad_k, grad_v)

def one_section(pair):
    arrived, dout = pair
    query = arrived[:, 0].transpose(1, 0, 2)
    keys = arrived[:, 1].transpose(1, 0, 2)
    values = arrived[:, 2].transpose(1, 0, 2)
    cotan = dout.transpose(1, 0, 2)
    output, grad_q, grad_k, grad_v = jax.vmap(head_pass)(query, keys, values, cotan)
    output = output.transpose(1, 0, 2).reshape(LEN, D)
    grads = jnp.stack([grad_q, grad_k, grad_v], axis=0).transpose(2, 0, 1, 3).reshape(LEN, 3, D)
    return (output, grads)

def reference(qkv_sent, grad_out):
    incoming = jnp.roll(qkv_sent, 1, axis=0).reshape(SECTIONS, LEN, 3, HEADS, HD)
    cotan = grad_out.reshape(SECTIONS, LEN, HEADS, HD)
    attn_out, grads = lax.map(one_section, (incoming, cotan))
    grad_qkv = jnp.roll(grads, -1, axis=0)
    return (attn_out, grad_qkv)
```

```python
import math
import functools
import jax
import jax.numpy as jnp
from jax import lax
from jax.experimental import pallas as pl
from jax.experimental.pallas import tpu as pltpu
from jax.sharding import PartitionSpec as P

HD = 128
BLK = 256


def from_behind(value, axis, steps):
    count = lax.axis_size(axis)
    pairs = [(source, (source + steps) % count) for source in range(count)]
    return lax.ppermute(value, axis, pairs)


def dot_nt(a, b):
    return lax.dot_general(a, b, (((1,), (1,)), ((), ())), preferred_element_type=jnp.float32)


def dot_nn(a, b):
    return lax.dot_general(a, b, (((1,), (0,)), ((), ())), preferred_element_type=jnp.float32)


def dot_tn(a, b):
    return lax.dot_general(a, b, (((0,), (0,)), ((), ())), preferred_element_type=jnp.float32)


def probabilities(query, keys, first):
    scores = dot_nt(query, keys)
    rows = lax.broadcasted_iota(jnp.int32, scores.shape, 0) + first
    cols = lax.broadcasted_iota(jnp.int32, scores.shape, 1)
    scores = jnp.where(cols <= rows, scores, -jnp.inf)
    peak = jnp.max(scores, axis=1, keepdims=True)
    expo = jnp.exp2((scores - peak) * (math.log2(math.e) / math.sqrt(HD)))
    return expo * (1.0 / jnp.sum(expo, axis=1, keepdims=True))


def forward_kernel(qkv_ref, out_ref, weights_ref):
    length, width = out_ref.shape
    for head in range(width // HD):
        at = slice(head * HD, (head + 1) * HD)
        for first in range(0, length, BLK):
            q_at, k_at = slice(first, first + BLK), slice(0, first + BLK)
            probs = probabilities(qkv_ref[0, q_at, at], qkv_ref[1, k_at, at], first)
            weights = probs.astype(jnp.bfloat16)
            weights_ref[head, q_at, k_at] = weights
            out_ref[q_at, at] = dot_nn(weights, qkv_ref[2, k_at, at]).astype(jnp.bfloat16)


def backward_kernel(qkv_ref, weights_ref, out_ref, dout_ref, grads_ref):
    length, width = out_ref.shape
    scale = 1.0 / math.sqrt(HD)
    for head in range(width // HD):
        at = slice(head * HD, (head + 1) * HD)
        dk = [None] * (length // BLK)
        dv = [None] * (length // BLK)
        for i in range(length // BLK):
            q_at, k_at = slice(i * BLK, (i + 1) * BLK), slice(0, (i + 1) * BLK)
            dout = dout_ref[q_at, at]
            delta = jnp.sum(dout.astype(jnp.float32) * out_ref[q_at, at].astype(jnp.float32), axis=1, keepdims=True)
            weights = weights_ref[head, q_at, k_at]
            grad_p = dot_nt(dout, qkv_ref[2, k_at, at])
            grad_s = (weights.astype(jnp.float32) * (grad_p - delta)).astype(jnp.bfloat16)
            grads_ref[0, q_at, at] = (dot_nn(grad_s, qkv_ref[1, k_at, at]) * scale).astype(jnp.bfloat16)
            query = qkv_ref[0, q_at, at]
            for j in range(i + 1):
                sub = slice(j * BLK, (j + 1) * BLK)
                kk = dot_tn(grad_s[:, sub], query)
                vv = dot_tn(weights[:, sub], dout)
                dk[j] = kk if dk[j] is None else dk[j] + kk
                dv[j] = vv if dv[j] is None else dv[j] + vv
        for j in range(length // BLK):
            sub = slice(j * BLK, (j + 1) * BLK)
            grads_ref[1, sub, at] = (dk[j] * scale).astype(jnp.bfloat16)
            grads_ref[2, sub, at] = dv[j].astype(jnp.bfloat16)


VMEM = pl.BlockSpec(memory_space=pltpu.VMEM)


def forward(qkv):
    _, length, width = qkv.shape
    heads = width // HD
    return pl.pallas_call(
        forward_kernel,
        out_shape=(
            jax.ShapeDtypeStruct((length, width), jnp.bfloat16),
            jax.ShapeDtypeStruct((heads, length, length), jnp.bfloat16),
        ),
        in_specs=[VMEM],
        out_specs=(VMEM, VMEM),
        name="forward",
        compiler_params=pltpu.CompilerParams(vmem_limit_bytes=24 * 2**20),
        cost_estimate=pl.CostEstimate(
            flops=4 * heads * length * length * HD, bytes_accessed=4 * length * width * 2, transcendentals=heads * length * length
        ),
    )(qkv)


def backward(qkv, weights, out, dout):
    _, length, width = qkv.shape
    heads = width // HD
    return pl.pallas_call(
        backward_kernel,
        out_shape=jax.ShapeDtypeStruct(qkv.shape, jnp.bfloat16),
        in_specs=[VMEM] * 4,
        out_specs=VMEM,
        name="backward",
        compiler_params=pltpu.CompilerParams(vmem_limit_bytes=24 * 2**20),
        cost_estimate=pl.CostEstimate(
            flops=8 * heads * length * length * HD, bytes_accessed=9 * length * width * 2, transcendentals=0
        ),
    )(qkv, weights, out, dout)


def on_device(qkv_sent, grad_out):
    qkv = qkv_sent[0].transpose(1, 0, 2)
    dout = from_behind(grad_out[0], "section", -1)
    out, weights = forward(qkv)
    attn_out = from_behind(out, "section", 1)
    grads = backward(qkv, weights, out, dout)
    return (attn_out[None], grads.transpose(1, 0, 2)[None])


def solution(mesh):
    in_specs = (P("section", None, None, "tp"), P("section", None, "tp"))
    out_specs = (P("section", None, "tp"), P("section", None, None, "tp"))
    return jax.shard_map(
        on_device, mesh=mesh, in_specs=in_specs, out_specs=out_specs, check_vma=False
    )
```

```python
import math
import jax
import jax.numpy as jnp
from jax import lax
from jax.experimental import pallas as pl
from jax.experimental.pallas import tpu as pltpu
from jax.sharding import PartitionSpec as P

HD = 128
BLK = 256
SECTION = "section"
FACTOR = math.log2(math.e) / math.sqrt(HD)
SCALE = 1.0 / math.sqrt(HD)


def near_pairs(count, half, steps):
    pairs = [(source, (source + steps) % count) for source in range(count)]
    return [(source, target) for source, target in pairs if source // half == target // half]


def far_pairs(count, half, moves):
    return [
        (base + source, (base + half + target) % count)
        for base in range(0, count, half)
        for source, target in moves
    ]


def same_pairs(count, half, moves):
    return [(base + source, base + target) for base in range(0, count, half) for source, target in moves]


def dot_nt(a, b):
    return lax.dot_general(a, b, (((1,), (1,)), ((), ())), preferred_element_type=jnp.float32)


def dot_nn(a, b):
    return lax.dot_general(a, b, (((1,), (0,)), ((), ())), preferred_element_type=jnp.float32)


def dot_tn(a, b):
    return lax.dot_general(a, b, (((0,), (0,)), ((), ())), preferred_element_type=jnp.float32)


def lanes(head, wide=1):
    return slice(head * HD * wide, (head + 1) * HD * wide)


def forward_kernel(half, qkv_ref, dout_ref, out_ref, relay_ref, direct_ref, expo_ref, inverse_ref, values_ref):
    length, width = out_ref.shape
    heads = width // HD
    cut = relay_ref.shape[0]
    for head in range(heads):
        values_ref[:, 2 * head * HD : (2 * head + 1) * HD] = qkv_ref[2, :, lanes(head)]
        values_ref[:, (2 * head + 1) * HD : (2 * head + 2) * HD] = jnp.ones((length, HD), jnp.bfloat16)
    for first in range(0, length, BLK):
        q_at, k_at = slice(first, first + BLK), slice(0, first + BLK)
        for head in range(heads):
            at = lanes(head)
            scores = dot_nt(qkv_ref[0, q_at, at], qkv_ref[1, k_at, at])
            rows = lax.broadcasted_iota(jnp.int32, scores.shape, 0) + first
            cols = lax.broadcasted_iota(jnp.int32, scores.shape, 1)
            scores = jnp.where(cols <= rows, scores, -jnp.inf)
            peak = jnp.max(scores, axis=1, keepdims=True)
            expo = jnp.exp2((scores - peak) * FACTOR).astype(jnp.bfloat16)
            expo_ref[head, q_at, k_at] = expo
            both = dot_nn(expo, values_ref[k_at, lanes(head, 2)])
            inverse = 1.0 / both[:, HD:]
            inverse_ref[q_at, at] = inverse
            out_ref[q_at, at] = (both[:, :HD] * inverse).astype(jnp.bfloat16)
    sends_dout = lax.rem(lax.axis_index(SECTION), half) == 0

    @pl.when(sends_dout)
    def _():
        relay_ref[...] = dout_ref[0:cut]
        direct_ref[...] = dout_ref[cut:length]

    @pl.when(jnp.logical_not(sends_dout))
    def _():
        relay_ref[...] = out_ref[0:cut]
        direct_ref[...] = out_ref[cut:length]


def backward_kernel(
    half,
    qkv_ref,
    expo_ref,
    inverse_ref,
    values_ref,
    out_ref,
    near_dout_ref,
    near_out_ref,
    relay_ref,
    direct_ref,
    attn_ref,
    grads_ref,
    dout_ref,
    stage_ref,
    attn_sem,
    grads_sem,
):
    length, width = out_ref.shape
    heads = width // HD
    cut = relay_ref.shape[0]
    place = lax.rem(lax.axis_index(SECTION), half)
    parts = ((0, cut, relay_ref), (cut, length, direct_ref))

    def send(source, k, start, stop):
        return pltpu.make_async_copy(source, attn_ref.at[start:stop], attn_sem.at[k])

    @pl.when(place == 0)
    def _():
        for k, (start, stop, ref) in enumerate(parts):
            send(ref, k, start, stop).start()

    @pl.when(place != 0)
    def _():
        for k, (start, stop, _) in enumerate(parts):
            send(near_out_ref.at[start:stop], k, start, stop).start()

    def prepare(start, stop, dout):
        for head in range(heads):
            at = lanes(head)
            scaled = dout[:, at].astype(jnp.float32) * inverse_ref[start:stop, at]
            dout_ref[start:stop, 2 * head * HD : (2 * head + 1) * HD] = scaled.astype(jnp.bfloat16)
            product = scaled * out_ref[start:stop, at].astype(jnp.float32)
            dout_ref[start:stop, (2 * head + 1) * HD : (2 * head + 2) * HD] = (-product).astype(jnp.bfloat16)

    @pl.when(place == half - 1)
    def _():
        for start, stop, ref in parts:
            prepare(start, stop, ref)

    @pl.when(place != half - 1)
    def _():
        prepare(0, length, near_dout_ref)

    n = length // BLK
    copies = []
    for head in range(heads):
        at, wide = lanes(head), lanes(head, 2)
        dk, dv = [None] * n, [None] * n
        for i in range(n):
            q_at, k_at = slice(i * BLK, (i + 1) * BLK), slice(0, (i + 1) * BLK)
            expo = expo_ref[head, q_at, k_at]
            grad_p = dot_nt(dout_ref[q_at, wide], values_ref[k_at, wide])
            grad_s = (expo.astype(jnp.float32) * grad_p).astype(jnp.bfloat16)
            stage_ref[0, q_at, at] = (dot_nn(grad_s, qkv_ref[1, k_at, at]) * SCALE).astype(jnp.bfloat16)
            for j in range(i + 1):
                sub = slice(j * BLK, (j + 1) * BLK)
                kk = dot_tn(grad_s[:, sub], qkv_ref[0, q_at, at])
                vv = dot_tn(expo[:, sub], dout_ref[q_at, 2 * head * HD : (2 * head + 1) * HD])
                dk[j] = kk if dk[j] is None else dk[j] + kk
                dv[j] = vv if dv[j] is None else dv[j] + vv
        for j in range(n):
            sub = slice(j * BLK, (j + 1) * BLK)
            stage_ref[1, sub, at] = (dk[j] * SCALE).astype(jnp.bfloat16)
            stage_ref[2, sub, at] = dv[j].astype(jnp.bfloat16)
        copy = pltpu.make_async_copy(stage_ref.at[:, :, at], grads_ref.at[:, :, at], grads_sem.at[head])
        copy.start()
        copies.append(copy)
    for copy in copies:
        copy.wait()
    for k, (start, stop, _) in enumerate(parts):
        send(near_out_ref.at[start:stop], k, start, stop).wait()


VMEM = pl.BlockSpec(memory_space=pltpu.VMEM)
ANY = pl.BlockSpec(memory_space=pl.ANY)


def on_device(qkv_sent, grad_out):
    bf16 = jnp.bfloat16
    qkv = qkv_sent[0].transpose(1, 0, 2)
    dout = grad_out[0]
    _, length, width = qkv.shape
    heads = width // HD
    cut = length // 2
    count = lax.axis_size(SECTION)
    half = count // 2
    last = half - 1
    work = heads * length * length * HD
    struct = jax.ShapeDtypeStruct
    params = pltpu.CompilerParams(vmem_limit_bytes=28 * 2**20)

    near_dout = lax.ppermute(dout, SECTION, near_pairs(count, half, -1))
    out, relay, direct, expo, inverse, values = pl.pallas_call(
        lambda *refs: forward_kernel(half, *refs),
        out_shape=(
            struct((length, width), bf16),
            struct((cut, width), bf16),
            struct((length - cut, width), bf16),
            struct((heads, length, length), bf16),
            struct((length, width), jnp.float32),
            struct((length, 2 * width), bf16),
        ),
        in_specs=[VMEM] * 2,
        out_specs=(VMEM,) * 6,
        name="forward",
        compiler_params=params,
        cost_estimate=pl.CostEstimate(flops=4 * work, bytes_accessed=12 * length * width, transcendentals=0),
    )(qkv, dout)
    relay = lax.ppermute(relay, SECTION, same_pairs(count, half, [(0, 2), (last, last - 2)]))
    near_out = lax.ppermute(out, SECTION, near_pairs(count, half, 1))
    relay, direct = lax.optimization_barrier((relay, direct))
    relay = lax.ppermute(relay, SECTION, far_pairs(count, half, [(2, last), (last - 2, 0)]))
    direct = lax.ppermute(direct, SECTION, far_pairs(count, half, [(0, last), (last, 0)]))
    attn_out, grads = pl.pallas_call(
        lambda *refs: backward_kernel(half, *refs),
        out_shape=(struct((length, width), bf16), struct(qkv.shape, bf16)),
        in_specs=[VMEM] * 5 + [VMEM] * 4,
        out_specs=(ANY, ANY),
        scratch_shapes=[
            pltpu.VMEM((length, 2 * width), bf16),
            pltpu.VMEM(qkv.shape, bf16),
            pltpu.SemaphoreType.DMA((2,)),
            pltpu.SemaphoreType.DMA((heads,)),
        ],
        name="backward",
        compiler_params=params,
        cost_estimate=pl.CostEstimate(flops=8 * work, bytes_accessed=18 * length * width, transcendentals=0),
    )(qkv, expo, inverse, values, out, near_dout, near_out, relay, direct)
    return (attn_out[None], grads.transpose(1, 0, 2)[None])


def solution(mesh):
    in_specs = (P("section", None, None, "tp"), P("section", None, "tp"))
    out_specs = (P("section", None, "tp"), P("section", None, None, "tp"))
    return jax.shard_map(
        on_device, mesh=mesh, in_specs=in_specs, out_specs=out_specs, check_vma=False
    )
```

```python
import math
import jax
import jax.numpy as jnp
from jax import lax
from jax.experimental import pallas as pl
from jax.experimental.pallas import tpu as pltpu
from jax.sharding import PartitionSpec as P

HD = 128
BLK = 256
SECTION = "section"
FACTOR = math.log2(math.e) / math.sqrt(HD)
SCALE = 1.0 / math.sqrt(HD)


def near_pairs(count, half, steps):
    pairs = [(source, (source + steps) % count) for source in range(count)]
    return [(source, target) for source, target in pairs if source // half == target // half]


def far_pairs(count, half, moves):
    return [
        (base + source, (base + half + target) % count)
        for base in range(0, count, half)
        for source, target in moves
    ]


def same_pairs(count, half, moves):
    return [(base + source, base + target) for base in range(0, count, half) for source, target in moves]


def dot_nt(a, b):
    return lax.dot_general(a, b, (((1,), (1,)), ((), ())), preferred_element_type=jnp.float32)


def dot_nn(a, b):
    return lax.dot_general(a, b, (((1,), (0,)), ((), ())), preferred_element_type=jnp.float32)


def dot_tn(a, b):
    return lax.dot_general(a, b, (((0,), (0,)), ((), ())), preferred_element_type=jnp.float32)


def lanes(head, wide=1):
    return slice(head * HD * wide, (head + 1) * HD * wide)


def attend(qkv_ref, values_ref, expo_ref, inverse_ref, out_ref, start, stop, base):
    q_at, k_at, own = slice(start, stop), slice(0, stop), slice(start - base, stop - base)
    for head in range(expo_ref.shape[0]):
        at = lanes(head)
        scores = dot_nt(qkv_ref[0, q_at, at], qkv_ref[1, k_at, at])
        rows = lax.broadcasted_iota(jnp.int32, scores.shape, 0) + start
        cols = lax.broadcasted_iota(jnp.int32, scores.shape, 1)
        scores = jnp.where(cols <= rows, scores, -jnp.inf)
        peak = jnp.max(scores, axis=1, keepdims=True)
        expo = jnp.exp2((scores - peak) * FACTOR).astype(jnp.bfloat16)
        expo_ref[head, own, k_at] = expo
        both = dot_nn(expo, values_ref[k_at, lanes(head, 2)])
        inverse = 1.0 / both[:, HD:]
        inverse_ref[own, at] = inverse
        out_ref[q_at, at] = (both[:, :HD] * inverse).astype(jnp.bfloat16)


def set_values(qkv_ref, values_ref, start, stop):
    for head in range(qkv_ref.shape[2] // HD):
        values_ref[start:stop, 2 * head * HD : (2 * head + 1) * HD] = qkv_ref[2, start:stop, lanes(head)]
        values_ref[start:stop, (2 * head + 1) * HD : (2 * head + 2) * HD] = jnp.ones((stop - start, HD), jnp.bfloat16)


def first_kernel(
    half,
    qkv_hbm,
    dout_hbm,
    out_ref,
    relay_ref,
    expo_ref,
    inverse_ref,
    qkv_ref,
    dout_ref,
    values_ref,
    qkv_sem,
    dout_sem,
):
    cut = relay_ref.shape[0]
    length = qkv_ref.shape[1]
    chunks = []
    for k, (start, stop) in enumerate(((0, BLK), (BLK, cut), (cut, length))):
        chunks.append(pltpu.make_async_copy(qkv_hbm.at[:, start:stop], qkv_ref.at[:, start:stop], qkv_sem.at[k]))
    fetch = pltpu.make_async_copy(dout_hbm, dout_ref, dout_sem)
    chunks[0].start()
    chunks[1].start()
    fetch.start()
    chunks[2].start()
    for k, (start, stop) in enumerate(((0, BLK), (BLK, cut))):
        chunks[k].wait()
        set_values(qkv_ref, values_ref, start, stop)
        attend(qkv_ref, values_ref, expo_ref, inverse_ref, out_ref, start, stop, 0)
    rest = expo_ref.shape[2] - cut
    expo_ref[:, BLK:cut, cut:] = jnp.zeros((expo_ref.shape[0], cut - BLK, rest), jnp.bfloat16)
    fetch.wait()
    sends_dout = lax.rem(lax.axis_index(SECTION), half) == 0

    @pl.when(sends_dout)
    def _():
        relay_ref[...] = dout_ref[0:cut]

    @pl.when(jnp.logical_not(sends_dout))
    def _():
        relay_ref[...] = out_ref[...]

    chunks[2].wait()


def second_kernel(half, qkv_ref, dout_ref, early_ref, out_ref, direct_ref, expo_ref, inverse_ref, values_ref):
    length, width = out_ref.shape
    cut = early_ref.shape[0]
    set_values(qkv_ref, values_ref, 0, length)
    out_ref[0:cut] = early_ref[...]
    for start, stop in ((cut, 2 * BLK), (2 * BLK, length)):
        attend(qkv_ref, values_ref, expo_ref, inverse_ref, out_ref, start, stop, cut)
    sends_dout = lax.rem(lax.axis_index(SECTION), half) == 0

    @pl.when(sends_dout)
    def _():
        direct_ref[...] = dout_ref[cut:length]

    @pl.when(jnp.logical_not(sends_dout))
    def _():
        direct_ref[...] = out_ref[cut:length]


def gradients(refs, parts, grads_ref, dout_ref, stage_ref, grads_sem):
    qkv_ref, early_ref, late_ref, values_ref, out_ref = refs
    length, width = out_ref.shape
    heads = width // HD
    cut = early_ref.shape[1]
    n = length // BLK
    copies = []

    def expo_of(head, i, cols):
        start, stop = i * BLK, (i + 1) * BLK
        pieces = []
        if start < cut:
            pieces.append(early_ref[head, start : min(stop, cut), cols])
        if stop > cut:
            pieces.append(late_ref[head, max(start, cut) - cut : stop - cut, cols])
        return pieces[0] if len(pieces) == 1 else jnp.concatenate(pieces, axis=0)

    for head in range(heads):
        at, wide = lanes(head), lanes(head, 2)
        left = slice(2 * head * HD, (2 * head + 1) * HD)
        right = slice((2 * head + 1) * HD, (2 * head + 2) * HD)
        for start, stop, inverse_ref, ref in parts:
            scaled = ref[:, at].astype(jnp.float32) * inverse_ref[:, at]
            dout_ref[start:stop, left] = scaled.astype(jnp.bfloat16)
            product = scaled * out_ref[start:stop, at].astype(jnp.float32)
            dout_ref[start:stop, right] = (-product).astype(jnp.bfloat16)
        dk, dv = [None] * n, [None] * n
        for i in range(n):
            q_at, k_at = slice(i * BLK, (i + 1) * BLK), slice(0, (i + 1) * BLK)
            expo = expo_of(head, i, k_at)
            grad_p = dot_nt(dout_ref[q_at, wide], values_ref[k_at, wide])
            grad_s = (expo.astype(jnp.float32) * grad_p).astype(jnp.bfloat16)
            stage_ref[0, q_at, at] = (dot_nn(grad_s, qkv_ref[1, k_at, at]) * SCALE).astype(jnp.bfloat16)
            for j in range(i + 1):
                sub = slice(j * BLK, (j + 1) * BLK)
                kk = dot_tn(grad_s[:, sub], qkv_ref[0, q_at, at])
                vv = dot_tn(expo[:, sub], dout_ref[q_at, left])
                dk[j] = kk if dk[j] is None else dk[j] + kk
                dv[j] = vv if dv[j] is None else dv[j] + vv
        for j in range(n):
            sub = slice(j * BLK, (j + 1) * BLK)
            stage_ref[1, sub, at] = (dk[j] * SCALE).astype(jnp.bfloat16)
            stage_ref[2, sub, at] = dv[j].astype(jnp.bfloat16)
        copy = pltpu.make_async_copy(stage_ref.at[:, :, at], grads_ref.at[:, :, at], grads_sem.at[head])
        copy.start()
        copies.append(copy)
    for copy in copies:
        copy.wait()


def near_kernel(half, *refs):
    held, (first_ref, second_ref), (near_ref, _, grads_ref, passed_ref), work = refs[:5], refs[5:7], refs[7:11], refs[11:]
    cut, length = first_ref.shape[0], near_ref.shape[0]
    passed_ref[...] = held[4][...]

    @pl.when(lax.rem(lax.axis_index(SECTION), half) != half - 1)
    def _():
        parts = [(0, cut, first_ref, near_ref.at[0:cut]), (cut, length, second_ref, near_ref.at[cut:length])]
        gradients(held, parts, grads_ref, *work)


def far_kernel(half, _, *refs):
    held, (first_ref, second_ref, relay_ref, direct_ref, grads_ref, token_ref), work = refs[:5], refs[5:11], refs[11:]
    token_ref[...] = jnp.zeros_like(token_ref)
    cut, length = first_ref.shape[0], held[4].shape[0]

    @pl.when(lax.rem(lax.axis_index(SECTION), half) == half - 1)
    def _():
        parts = [(0, cut, first_ref, relay_ref), (cut, length, second_ref, direct_ref)]
        gradients(held, parts, grads_ref, *work)


def emit_kernel(half, _, near_ref, relay_ref, direct_ref, attn_ref, sem):
    cut, length = relay_ref.shape[0], attn_ref.shape[0]
    place = lax.rem(lax.axis_index(SECTION), half)
    parts = [(0, cut, relay_ref), (cut, length, direct_ref)]

    def send(k, source):
        return pltpu.make_async_copy(source, attn_ref.at[parts[k][0] : parts[k][1]], sem.at[k])

    @pl.when(place == 0)
    def _():
        for k, part in enumerate(parts):
            send(k, part[2]).start()

    @pl.when(place != 0)
    def _():
        for k, part in enumerate(parts):
            send(k, near_ref.at[part[0] : part[1]]).start()

    for k, part in enumerate(parts):
        send(k, near_ref.at[part[0] : part[1]]).wait()


VMEM = pl.BlockSpec(memory_space=pltpu.VMEM)
HBM = pl.BlockSpec(memory_space=pltpu.HBM)
ANY = pl.BlockSpec(memory_space=pl.ANY)
FIRST_LIMIT = 48 * 2**20


def on_device(qkv_sent, grad_out):
    bf16 = jnp.bfloat16
    qkv = qkv_sent[0].transpose(1, 0, 2)
    dout = grad_out[0]
    _, length, width = qkv.shape
    heads = width // HD
    cut = length // 2
    count = lax.axis_size(SECTION)
    half = count // 2
    last = half - 1
    work = heads * length * length * HD
    whole = jax.ShapeDtypeStruct((length, width), bf16)
    part = jax.ShapeDtypeStruct((cut, width), bf16)
    three = jax.ShapeDtypeStruct(qkv.shape, bf16)
    inverse = jax.ShapeDtypeStruct((cut, width), jnp.float32)
    params = pltpu.CompilerParams(vmem_limit_bytes=24 * 2**20)
    scratch = [
        pltpu.VMEM((length, 2 * width), bf16),
        pltpu.VMEM(qkv.shape, bf16),
        pltpu.SemaphoreType.DMA((heads,)),
    ]

    def cost(flops):
        return pl.CostEstimate(flops=flops, bytes_accessed=12 * length * width, transcendentals=0)

    early_out, relay, early, inverse0, held, held_dout = pl.pallas_call(
        lambda *refs: first_kernel(half, *refs),
        out_shape=(part, part, jax.ShapeDtypeStruct((heads, cut, 2 * BLK), bf16), inverse, three, whole),
        in_specs=[HBM] * 2,
        out_specs=(VMEM,) * 6,
        scratch_shapes=[
            pltpu.VMEM((cut, 2 * width), bf16),
            pltpu.SemaphoreType.DMA((3,)),
            pltpu.SemaphoreType.DMA,
        ],
        name="first",
        compiler_params=pltpu.CompilerParams(vmem_limit_bytes=FIRST_LIMIT),
        cost_estimate=cost(work),
    )(qkv, dout)
    relay = lax.ppermute(relay, SECTION, same_pairs(count, half, [(0, 2), (last, last - 2)]))
    near_dout = lax.ppermute(held_dout, SECTION, near_pairs(count, half, -1))
    out, direct, late, inverse1, values = pl.pallas_call(
        lambda *refs: second_kernel(half, *refs),
        out_shape=(
            whole,
            part,
            jax.ShapeDtypeStruct((heads, length - cut, length), bf16),
            inverse,
            jax.ShapeDtypeStruct((length, 2 * width), bf16),
        ),
        in_specs=[VMEM] * 3,
        out_specs=(VMEM,) * 5,
        name="second",
        compiler_params=params,
        cost_estimate=cost(40 * work),
    )(held, held_dout, early_out)
    relay_hop = relay
    relay, direct = lax.optimization_barrier((relay, direct))
    relay = lax.ppermute(relay, SECTION, far_pairs(count, half, [(2, last), (last - 2, 0)]))
    direct = lax.ppermute(direct, SECTION, far_pairs(count, half, [(0, last), (last, 0)]))
    kept = (held, early, late, values, out, inverse0, inverse1)
    grads, passed = pl.pallas_call(
        lambda *refs: near_kernel(half, *refs),
        out_shape=(three, whole),
        in_specs=[VMEM] * 8 + [ANY],
        out_specs=(HBM, VMEM),
        scratch_shapes=scratch,
        name="near",
        compiler_params=params,
        cost_estimate=cost(4 * work),
    )(*kept, near_dout, relay_hop)
    near_out = lax.ppermute(passed, SECTION, near_pairs(count, half, 1))
    grads, token = pl.pallas_call(
        lambda *refs: far_kernel(half, *refs),
        out_shape=(three, jax.ShapeDtypeStruct((8, HD), jnp.float32)),
        in_specs=[HBM] + [VMEM] * 9,
        out_specs=(HBM, VMEM),
        scratch_shapes=scratch,
        input_output_aliases={0: 0},
        name="far",
        compiler_params=params,
        cost_estimate=cost(40 * work),
    )(grads, *kept, relay, direct)
    attn_out = pl.pallas_call(
        lambda *refs: emit_kernel(half, *refs),
        out_shape=whole,
        in_specs=[ANY] * 4,
        out_specs=HBM,
        scratch_shapes=[pltpu.SemaphoreType.DMA((2,))],
        name="emit",
        compiler_params=pltpu.CompilerParams(vmem_limit_bytes=2**20),
        cost_estimate=cost(1),
    )(token, near_out, relay, direct)
    return (attn_out[None], grads.transpose(1, 0, 2)[None])


def solution(mesh):
    in_specs = (P("section", None, None, "tp"), P("section", None, "tp"))
    out_specs = (P("section", None, "tp"), P("section", None, None, "tp"))
    return jax.shard_map(
        on_device, mesh=mesh, in_specs=in_specs, out_specs=out_specs, check_vma=False
    )
```

```python
import math
import jax
import jax.numpy as jnp
from jax import lax
from jax.experimental import pallas as pl
from jax.experimental.pallas import tpu as pltpu
from jax.sharding import PartitionSpec as P

HD = 128
BLK = 256
SECTION = "section"
FACTOR = math.log2(math.e) / math.sqrt(HD)
SCALE = 1.0 / math.sqrt(HD)


def near_pairs(count, half, steps):
    pairs = [(source, (source + steps) % count) for source in range(count)]
    return [(source, target) for source, target in pairs if source // half == target // half]


def far_pairs(count, half, moves):
    return [
        (base + source, (base + half + target) % count)
        for base in range(0, count, half)
        for source, target in moves
    ]


def same_pairs(count, half, moves):
    return [(base + source, base + target) for base in range(0, count, half) for source, target in moves]


def dot_nt(a, b):
    return lax.dot_general(a, b, (((1,), (1,)), ((), ())), preferred_element_type=jnp.float32)


def dot_nn(a, b):
    return lax.dot_general(a, b, (((1,), (0,)), ((), ())), preferred_element_type=jnp.float32)


def dot_tn(a, b):
    return lax.dot_general(a, b, (((0,), (0,)), ((), ())), preferred_element_type=jnp.float32)


def lanes(head, wide=1):
    return slice(head * HD * wide, (head + 1) * HD * wide)


def attend(qkv_ref, values_ref, expo_ref, inverse_ref, out_ref, start, stop, base):
    q_at, k_at, own = slice(start, stop), slice(0, stop), slice(start - base, stop - base)
    for head in range(expo_ref.shape[0]):
        at = lanes(head)
        scores = dot_nt(qkv_ref[0, q_at, at], qkv_ref[1, k_at, at])
        rows = lax.broadcasted_iota(jnp.int32, scores.shape, 0) + start
        cols = lax.broadcasted_iota(jnp.int32, scores.shape, 1)
        scores = jnp.where(cols <= rows, scores, -jnp.inf)
        peak = jnp.max(scores, axis=1, keepdims=True)
        expo = jnp.exp2((scores - peak) * FACTOR).astype(jnp.bfloat16)
        expo_ref[head, own, k_at] = expo
        both = dot_nn(expo, values_ref[k_at, lanes(head, 2)])
        inverse = 1.0 / both[:, HD:]
        inverse_ref[own, at] = inverse
        out_ref[q_at, at] = (both[:, :HD] * inverse).astype(jnp.bfloat16)


def set_values(qkv_ref, values_ref, start, stop):
    for head in range(qkv_ref.shape[2] // HD):
        values_ref[start:stop, 2 * head * HD : (2 * head + 1) * HD] = qkv_ref[2, start:stop, lanes(head)]
        values_ref[start:stop, (2 * head + 1) * HD : (2 * head + 2) * HD] = jnp.ones((stop - start, HD), jnp.bfloat16)


def first_kernel(qkv_hbm, out_ref, expo_ref, inverse_ref, qkv_ref, values_ref, qkv_sem):
    cut = out_ref.shape[0]
    length = qkv_ref.shape[1]
    chunks = []
    for k, (start, stop) in enumerate(((0, BLK), (BLK, cut), (cut, length))):
        chunks.append(pltpu.make_async_copy(qkv_hbm.at[:, start:stop], qkv_ref.at[:, start:stop], qkv_sem.at[k]))
        chunks[k].start()
    for k, (start, stop) in enumerate(((0, BLK), (BLK, cut))):
        chunks[k].wait()
        set_values(qkv_ref, values_ref, start, stop)
        attend(qkv_ref, values_ref, expo_ref, inverse_ref, out_ref, start, stop, 0)
    rest = expo_ref.shape[2] - cut
    expo_ref[:, BLK:cut, cut:] = jnp.zeros((expo_ref.shape[0], cut - BLK, rest), jnp.bfloat16)
    chunks[2].wait()


def pick_kernel(half, out_ref, dout_ref, relay_ref, held_ref):
    sends_dout = lax.rem(lax.axis_index(SECTION), half) == 0
    held_ref[...] = dout_ref[...]

    @pl.when(sends_dout)
    def _():
        relay_ref[...] = dout_ref[0 : relay_ref.shape[0]]

    @pl.when(jnp.logical_not(sends_dout))
    def _():
        relay_ref[...] = out_ref[...]


def second_kernel(half, qkv_ref, dout_ref, early_ref, out_ref, direct_ref, expo_ref, inverse_ref, values_ref):
    length, width = out_ref.shape
    cut = early_ref.shape[0]
    set_values(qkv_ref, values_ref, 0, length)
    out_ref[0:cut] = early_ref[...]
    for start, stop in ((cut, 2 * BLK), (2 * BLK, length)):
        attend(qkv_ref, values_ref, expo_ref, inverse_ref, out_ref, start, stop, cut)
    sends_dout = lax.rem(lax.axis_index(SECTION), half) == 0

    @pl.when(sends_dout)
    def _():
        direct_ref[...] = dout_ref[cut:length]

    @pl.when(jnp.logical_not(sends_dout))
    def _():
        direct_ref[...] = out_ref[cut:length]


def gradients(refs, parts, grads_ref, dout_ref, stage_ref, scores_ref, sums_ref, grads_sem):
    qkv_ref, early_ref, late_ref, values_ref, out_ref = refs
    length, width = out_ref.shape
    heads = width // HD
    cut = early_ref.shape[1]
    copies = []

    def expo_of(head, start, stop, cols):
        pieces = []
        if start < cut:
            pieces.append(early_ref[head, start : min(stop, cut), cols])
        if stop > cut:
            pieces.append(late_ref[head, max(start, cut) - cut : stop - cut, cols])
        return pieces[0] if len(pieces) == 1 else jnp.concatenate(pieces, axis=0)

    for head in range(heads):
        at, wide = lanes(head), lanes(head, 2)
        left = slice(2 * head * HD, (2 * head + 1) * HD)
        right = slice((2 * head + 1) * HD, (2 * head + 2) * HD)
        for start, stop, inverse_ref, ref in parts:
            scaled = ref[:, at].astype(jnp.float32) * inverse_ref[:, at]
            dout_ref[start:stop, left] = scaled.astype(jnp.bfloat16)
            product = scaled * out_ref[start:stop, at].astype(jnp.float32)
            dout_ref[start:stop, right] = (-product).astype(jnp.bfloat16)
        for first in range(0, length, BLK):
            k_at, q_at = slice(first, first + BLK), slice(first, length)
            grad_p = dot_nt(dout_ref[q_at, wide], values_ref[k_at, wide])
            expo = expo_of(head, first, length, k_at)
            grad_s = (expo.astype(jnp.float32) * grad_p).astype(jnp.bfloat16)
            scores_ref[q_at, k_at] = grad_s
            dq = dot_nn(grad_s, qkv_ref[1, k_at, at])
            sums_ref[0, q_at] = dq if first == 0 else sums_ref[0, q_at] + dq
        stage_ref[0, :, at] = (sums_ref[0] * SCALE).astype(jnp.bfloat16)
        for first in reversed(range(0, length, BLK)):
            q_at, k_at = slice(first, first + BLK), slice(0, first + BLK)
            dk = dot_tn(scores_ref[q_at, k_at], qkv_ref[0, q_at, at])
            dv = dot_tn(expo_of(head, first, first + BLK, k_at), dout_ref[q_at, left])
            last = first + BLK == length
            sums_ref[1, k_at] = dk if last else sums_ref[1, k_at] + dk
            sums_ref[2, k_at] = dv if last else sums_ref[2, k_at] + dv
        stage_ref[1, :, at] = (sums_ref[1] * SCALE).astype(jnp.bfloat16)
        stage_ref[2, :, at] = sums_ref[2].astype(jnp.bfloat16)
        copy = pltpu.make_async_copy(stage_ref.at[:, :, at], grads_ref.at[:, :, at], grads_sem.at[head])
        copy.start()
        copies.append(copy)
    for copy in copies:
        copy.wait()


def near_kernel(half, *refs):
    held, (first_ref, second_ref), (near_ref, _, grads_ref, passed_ref), work = refs[:5], refs[5:7], refs[7:11], refs[11:]
    cut, length = first_ref.shape[0], near_ref.shape[0]
    passed_ref[...] = held[4][...]

    @pl.when(lax.rem(lax.axis_index(SECTION), half) != half - 1)
    def _():
        parts = [(0, cut, first_ref, near_ref.at[0:cut]), (cut, length, second_ref, near_ref.at[cut:length])]
        gradients(held, parts, grads_ref, *work)


def far_kernel(half, _, *refs):
    held, (first_ref, second_ref, relay_ref, direct_ref, grads_ref, token_ref), work = refs[:5], refs[5:11], refs[11:]
    token_ref[...] = jnp.zeros_like(token_ref)
    cut, length = first_ref.shape[0], held[4].shape[0]

    @pl.when(lax.rem(lax.axis_index(SECTION), half) == half - 1)
    def _():
        parts = [(0, cut, first_ref, relay_ref), (cut, length, second_ref, direct_ref)]
        gradients(held, parts, grads_ref, *work)


def emit_kernel(half, _, near_ref, relay_ref, direct_ref, attn_ref, sem):
    cut, length = relay_ref.shape[0], attn_ref.shape[0]
    place = lax.rem(lax.axis_index(SECTION), half)
    parts = [(0, cut, relay_ref), (cut, length, direct_ref)]

    def send(k, source):
        return pltpu.make_async_copy(source, attn_ref.at[parts[k][0] : parts[k][1]], sem.at[k])

    @pl.when(place == 0)
    def _():
        for k, part in enumerate(parts):
            send(k, part[2]).start()

    @pl.when(place != 0)
    def _():
        for k, part in enumerate(parts):
            send(k, near_ref.at[part[0] : part[1]]).start()

    for k, part in enumerate(parts):
        send(k, near_ref.at[part[0] : part[1]]).wait()


VMEM = pl.BlockSpec(memory_space=pltpu.VMEM)
HBM = pl.BlockSpec(memory_space=pltpu.HBM)
ANY = pl.BlockSpec(memory_space=pl.ANY)
FIRST_LIMIT = 49 * 2**20


def on_device(qkv_sent, grad_out):
    bf16 = jnp.bfloat16
    qkv = qkv_sent[0].transpose(1, 0, 2)
    dout = grad_out[0]
    _, length, width = qkv.shape
    heads = width // HD
    cut = length // 2
    count = lax.axis_size(SECTION)
    half = count // 2
    last = half - 1
    work = heads * length * length * HD
    whole = jax.ShapeDtypeStruct((length, width), bf16)
    part = jax.ShapeDtypeStruct((cut, width), bf16)
    three = jax.ShapeDtypeStruct(qkv.shape, bf16)
    inverse = jax.ShapeDtypeStruct((cut, width), jnp.float32)
    params = pltpu.CompilerParams(vmem_limit_bytes=24 * 2**20)
    scratch = [
        pltpu.VMEM((length, 2 * width), bf16),
        pltpu.VMEM(qkv.shape, bf16),
        pltpu.VMEM((length, length), bf16),
        pltpu.VMEM((3, length, HD), jnp.float32),
        pltpu.SemaphoreType.DMA((heads,)),
    ]

    def cost(flops):
        return pl.CostEstimate(flops=flops, bytes_accessed=12 * length * width, transcendentals=0)

    early_out, early, inverse0, held = pl.pallas_call(
        first_kernel,
        out_shape=(part, jax.ShapeDtypeStruct((heads, cut, 2 * BLK), bf16), inverse, three),
        in_specs=[HBM],
        out_specs=(VMEM,) * 4,
        scratch_shapes=[pltpu.VMEM((cut, 2 * width), bf16), pltpu.SemaphoreType.DMA((3,))],
        name="first",
        compiler_params=pltpu.CompilerParams(vmem_limit_bytes=FIRST_LIMIT),
        cost_estimate=cost(work),
    )(qkv)
    relay, held_dout = pl.pallas_call(
        lambda *refs: pick_kernel(half, *refs),
        out_shape=(part, whole),
        in_specs=[VMEM] * 2,
        out_specs=(VMEM,) * 2,
        name="pick",
        compiler_params=pltpu.CompilerParams(vmem_limit_bytes=4 * 2**20),
        cost_estimate=cost(1),
    )(early_out, dout)
    relay = lax.ppermute(relay, SECTION, same_pairs(count, half, [(0, 2), (last, last - 2)]))
    near_dout = lax.ppermute(held_dout, SECTION, near_pairs(count, half, -1))
    out, direct, late, inverse1, values = pl.pallas_call(
        lambda *refs: second_kernel(half, *refs),
        out_shape=(
            whole,
            part,
            jax.ShapeDtypeStruct((heads, length - cut, length), bf16),
            inverse,
            jax.ShapeDtypeStruct((length, 2 * width), bf16),
        ),
        in_specs=[VMEM] * 3,
        out_specs=(VMEM,) * 5,
        name="second",
        compiler_params=params,
        cost_estimate=cost(40 * work),
    )(held, held_dout, early_out)
    relay_hop = relay
    relay, direct = lax.optimization_barrier((relay, direct))
    relay = lax.ppermute(relay, SECTION, far_pairs(count, half, [(2, last), (last - 2, 0)]))
    direct = lax.ppermute(direct, SECTION, far_pairs(count, half, [(0, last), (last, 0)]))
    kept = (held, early, late, values, out, inverse0, inverse1)
    grads, passed = pl.pallas_call(
        lambda *refs: near_kernel(half, *refs),
        out_shape=(three, whole),
        in_specs=[VMEM] * 8 + [ANY],
        out_specs=(HBM, VMEM),
        scratch_shapes=scratch,
        name="near",
        compiler_params=params,
        cost_estimate=cost(4 * work),
    )(*kept, near_dout, relay_hop)
    near_out = lax.ppermute(passed, SECTION, near_pairs(count, half, 1))
    grads, token = pl.pallas_call(
        lambda *refs: far_kernel(half, *refs),
        out_shape=(three, jax.ShapeDtypeStruct((8, HD), jnp.float32)),
        in_specs=[HBM] + [VMEM] * 9,
        out_specs=(HBM, VMEM),
        scratch_shapes=scratch,
        input_output_aliases={0: 0},
        name="far",
        compiler_params=params,
        cost_estimate=cost(40 * work),
    )(grads, *kept, relay, direct)
    attn_out = pl.pallas_call(
        lambda *refs: emit_kernel(half, *refs),
        out_shape=whole,
        in_specs=[ANY] * 4,
        out_specs=HBM,
        scratch_shapes=[pltpu.SemaphoreType.DMA((2,))],
        name="emit",
        compiler_params=pltpu.CompilerParams(vmem_limit_bytes=2**20),
        cost_estimate=cost(1),
    )(token, near_out, relay, direct)
    return (attn_out[None], grads.transpose(1, 0, 2)[None])


def solution(mesh):
    in_specs = (P("section", None, None, "tp"), P("section", None, "tp"))
    out_specs = (P("section", None, "tp"), P("section", None, None, "tp"))
    return jax.shard_map(
        on_device, mesh=mesh, in_specs=in_specs, out_specs=out_specs, check_vma=False
    )
```

```python
import math
import jax
import jax.numpy as jnp
from jax import lax
from jax.experimental import pallas as pl
from jax.experimental.pallas import tpu as pltpu
from jax.sharding import PartitionSpec as P

HD = 128
BLK = 256
SECTION = "section"
FACTOR = math.log2(math.e) / math.sqrt(HD)
SCALE = 1.0 / math.sqrt(HD)


def near_pairs(count, half, steps):
    pairs = [(source, (source + steps) % count) for source in range(count)]
    return [(source, target) for source, target in pairs if source // half == target // half]


def far_pairs(count, half, moves):
    return [
        (base + source, (base + half + target) % count)
        for base in range(0, count, half)
        for source, target in moves
    ]


def same_pairs(count, half, moves):
    return [(base + source, base + target) for base in range(0, count, half) for source, target in moves]


def dot_nt(a, b):
    return lax.dot_general(a, b, (((1,), (1,)), ((), ())), preferred_element_type=jnp.float32)


def dot_nn(a, b):
    return lax.dot_general(a, b, (((1,), (0,)), ((), ())), preferred_element_type=jnp.float32)


def dot_tn(a, b):
    return lax.dot_general(a, b, (((0,), (0,)), ((), ())), preferred_element_type=jnp.float32)


def lanes(head, wide=1):
    return slice(head * HD * wide, (head + 1) * HD * wide)


def attend(qkv_ref, values_ref, expo_ref, inverse_ref, out_ref, start, stop, base):
    q_at, k_at, own = slice(start, stop), slice(0, stop), slice(start - base, stop - base)
    for head in range(expo_ref.shape[0]):
        at = lanes(head)
        scores = dot_nt(qkv_ref[0, q_at, at], qkv_ref[1, k_at, at])
        rows = lax.broadcasted_iota(jnp.int32, scores.shape, 0) + start
        cols = lax.broadcasted_iota(jnp.int32, scores.shape, 1)
        scores = jnp.where(cols <= rows, scores, -jnp.inf)
        peak = jnp.max(scores, axis=1, keepdims=True)
        expo = jnp.exp2((scores - peak) * FACTOR).astype(jnp.bfloat16)
        expo_ref[head, own, k_at] = expo
        both = dot_nn(expo, values_ref[k_at, lanes(head, 2)])
        inverse = 1.0 / both[:, HD:]
        inverse_ref[own, at] = inverse
        out_ref[q_at, at] = (both[:, :HD] * inverse).astype(jnp.bfloat16)


def set_values(qkv_ref, values_ref, start, stop):
    for head in range(qkv_ref.shape[2] // HD):
        values_ref[start:stop, 2 * head * HD : (2 * head + 1) * HD] = qkv_ref[2, start:stop, lanes(head)]
        values_ref[start:stop, (2 * head + 1) * HD : (2 * head + 2) * HD] = jnp.ones((stop - start, HD), jnp.bfloat16)


def first_kernel(qkv_hbm, out_ref, expo_ref, inverse_ref, qkv_ref, values_ref, qkv_sem):
    cut = out_ref.shape[0]
    length = qkv_ref.shape[1]
    chunks = []
    for k, (start, stop) in enumerate(((0, BLK), (BLK, cut), (cut, length))):
        chunks.append(pltpu.make_async_copy(qkv_hbm.at[:, start:stop], qkv_ref.at[:, start:stop], qkv_sem.at[k]))
        chunks[k].start()
    for k, (start, stop) in enumerate(((0, BLK), (BLK, cut))):
        chunks[k].wait()
        set_values(qkv_ref, values_ref, start, stop)
        attend(qkv_ref, values_ref, expo_ref, inverse_ref, out_ref, start, stop, 0)
    rest = expo_ref.shape[2] - cut
    expo_ref[:, BLK:cut, cut:] = jnp.zeros((expo_ref.shape[0], cut - BLK, rest), jnp.bfloat16)
    chunks[2].wait()


def pick_kernel(half, out_ref, dout_ref, relay_ref, held_ref):
    sends_dout = lax.rem(lax.axis_index(SECTION), half) == 0
    held_ref[...] = dout_ref[...]

    @pl.when(sends_dout)
    def _():
        relay_ref[...] = dout_ref[0 : relay_ref.shape[0]]

    @pl.when(jnp.logical_not(sends_dout))
    def _():
        relay_ref[...] = out_ref[...]


def second_kernel(half, qkv_ref, dout_ref, early_ref, out_ref, direct_ref, expo_ref, inverse_ref, values_ref):
    length, width = out_ref.shape
    cut = early_ref.shape[0]
    set_values(qkv_ref, values_ref, 0, length)
    out_ref[0:cut] = early_ref[...]
    for start, stop in ((cut, 2 * BLK), (2 * BLK, length)):
        attend(qkv_ref, values_ref, expo_ref, inverse_ref, out_ref, start, stop, cut)
    sends_dout = lax.rem(lax.axis_index(SECTION), half) == 0

    @pl.when(sends_dout)
    def _():
        direct_ref[...] = dout_ref[cut:length]

    @pl.when(jnp.logical_not(sends_dout))
    def _():
        direct_ref[...] = out_ref[cut:length]


def gradients(refs, parts, grads_ref, dout_ref, stage_ref, scores_ref, sums_ref, grads_sem):
    qkv_ref, early_ref, late_ref, values_ref, out_ref = refs
    length, width = out_ref.shape
    heads = width // HD
    cut = early_ref.shape[1]
    copies = []

    def expo_of(head, start, stop, cols):
        pieces = []
        if start < cut:
            pieces.append(early_ref[head, start : min(stop, cut), cols])
        if stop > cut:
            pieces.append(late_ref[head, max(start, cut) - cut : stop - cut, cols])
        return pieces[0] if len(pieces) == 1 else jnp.concatenate(pieces, axis=0)

    for head in range(heads):
        at, wide = lanes(head), lanes(head, 2)
        left = slice(2 * head * HD, (2 * head + 1) * HD)
        right = slice((2 * head + 1) * HD, (2 * head + 2) * HD)
        for start, stop, inverse_ref, ref in parts:
            scaled = ref[:, at].astype(jnp.float32) * inverse_ref[:, at]
            dout_ref[start:stop, left] = scaled.astype(jnp.bfloat16)
            product = scaled * out_ref[start:stop, at].astype(jnp.float32)
            dout_ref[start:stop, right] = (-product).astype(jnp.bfloat16)
        for first in range(0, length, BLK):
            k_at, q_at = slice(first, first + BLK), slice(first, length)
            grad_p = dot_nt(dout_ref[q_at, wide], values_ref[k_at, wide])
            expo = expo_of(head, first, length, k_at)
            grad_s = (expo.astype(jnp.float32) * grad_p).astype(jnp.bfloat16)
            scores_ref[q_at, k_at] = grad_s
            dq = dot_nn(grad_s, qkv_ref[1, k_at, at])
            sums_ref[0, q_at] = dq if first == 0 else sums_ref[0, q_at] + dq
        stage_ref[0, :, at] = (sums_ref[0] * SCALE).astype(jnp.bfloat16)
        for first in reversed(range(0, length, BLK)):
            q_at, k_at = slice(first, first + BLK), slice(0, first + BLK)
            dk = dot_tn(scores_ref[q_at, k_at], qkv_ref[0, q_at, at])
            dv = dot_tn(expo_of(head, first, first + BLK, k_at), dout_ref[q_at, left])
            last = first + BLK == length
            sums_ref[1, k_at] = dk if last else sums_ref[1, k_at] + dk
            sums_ref[2, k_at] = dv if last else sums_ref[2, k_at] + dv
        stage_ref[1, :, at] = (sums_ref[1] * SCALE).astype(jnp.bfloat16)
        stage_ref[2, :, at] = sums_ref[2].astype(jnp.bfloat16)
        copy = pltpu.make_async_copy(stage_ref.at[:, :, at], grads_ref.at[:, :, at], grads_sem.at[head])
        copy.start()
        copies.append(copy)
    for copy in copies:
        copy.wait()


def near_kernel(half, *refs):
    held, (first_ref, second_ref), (near_ref, _, grads_ref, passed_ref), work = refs[:5], refs[5:7], refs[7:11], refs[11:]
    cut, length = first_ref.shape[0], near_ref.shape[0]
    passed_ref[...] = held[4][...]

    @pl.when(lax.rem(lax.axis_index(SECTION), half) != half - 1)
    def _():
        parts = [(0, cut, first_ref, near_ref.at[0:cut]), (cut, length, second_ref, near_ref.at[cut:length])]
        gradients(held, parts, grads_ref, *work)


def token_kernel(*refs):
    refs[-1][...] = jnp.zeros_like(refs[-1])


def far_kernel(half, _, __, *refs):
    held, (first_ref, second_ref, relay_ref, direct_ref, near_ref, grads_ref, attn_ref), work = refs[:5], refs[5:12], refs[12:]
    work, sem = work[:-1], work[-1]
    cut, length = first_ref.shape[0], attn_ref.shape[0]
    place = lax.rem(lax.axis_index(SECTION), half)
    parts = [(0, cut, first_ref, relay_ref), (cut, length, second_ref, direct_ref)]

    def send(k, source):
        return pltpu.make_async_copy(source, attn_ref.at[parts[k][0] : parts[k][1]], sem.at[k])

    @pl.when(place == 0)
    def _():
        for k, part in enumerate(parts):
            send(k, part[3]).start()

    @pl.when(place != 0)
    def _():
        for k, part in enumerate(parts):
            send(k, near_ref.at[part[0] : part[1]]).start()

    @pl.when(place == half - 1)
    def _():
        gradients(held, parts, grads_ref, *work)

    for k, part in enumerate(parts):
        send(k, near_ref.at[part[0] : part[1]]).wait()


VMEM = pl.BlockSpec(memory_space=pltpu.VMEM)
HBM = pl.BlockSpec(memory_space=pltpu.HBM)
ANY = pl.BlockSpec(memory_space=pl.ANY)
FIRST_LIMIT = 49 * 2**20


def on_device(qkv_sent, grad_out):
    bf16 = jnp.bfloat16
    qkv = qkv_sent[0].transpose(1, 0, 2)
    dout = grad_out[0]
    _, length, width = qkv.shape
    heads = width // HD
    cut = length // 2
    count = lax.axis_size(SECTION)
    half = count // 2
    last = half - 1
    work = heads * length * length * HD
    whole = jax.ShapeDtypeStruct((length, width), bf16)
    part = jax.ShapeDtypeStruct((cut, width), bf16)
    three = jax.ShapeDtypeStruct(qkv.shape, bf16)
    inverse = jax.ShapeDtypeStruct((cut, width), jnp.float32)
    params = pltpu.CompilerParams(vmem_limit_bytes=24 * 2**20)
    scratch = [
        pltpu.VMEM((length, 2 * width), bf16),
        pltpu.VMEM(qkv.shape, bf16),
        pltpu.VMEM((length, length), bf16),
        pltpu.VMEM((3, length, HD), jnp.float32),
        pltpu.SemaphoreType.DMA((heads,)),
    ]

    def cost(flops):
        return pl.CostEstimate(flops=flops, bytes_accessed=12 * length * width, transcendentals=0)

    early_out, early, inverse0, held = pl.pallas_call(
        first_kernel,
        out_shape=(part, jax.ShapeDtypeStruct((heads, cut, 2 * BLK), bf16), inverse, three),
        in_specs=[HBM],
        out_specs=(VMEM,) * 4,
        scratch_shapes=[pltpu.VMEM((cut, 2 * width), bf16), pltpu.SemaphoreType.DMA((3,))],
        name="first",
        compiler_params=pltpu.CompilerParams(vmem_limit_bytes=FIRST_LIMIT),
        cost_estimate=cost(work),
    )(qkv)
    relay, held_dout = pl.pallas_call(
        lambda *refs: pick_kernel(half, *refs),
        out_shape=(part, whole),
        in_specs=[VMEM] * 2,
        out_specs=(VMEM,) * 2,
        name="pick",
        compiler_params=pltpu.CompilerParams(vmem_limit_bytes=4 * 2**20),
        cost_estimate=cost(1),
    )(early_out, dout)
    relay = lax.ppermute(relay, SECTION, same_pairs(count, half, [(0, 2), (last, last - 2)]))
    near_dout = lax.ppermute(held_dout, SECTION, near_pairs(count, half, -1))
    out, direct, late, inverse1, values = pl.pallas_call(
        lambda *refs: second_kernel(half, *refs),
        out_shape=(
            whole,
            part,
            jax.ShapeDtypeStruct((heads, length - cut, length), bf16),
            inverse,
            jax.ShapeDtypeStruct((length, 2 * width), bf16),
        ),
        in_specs=[VMEM] * 3,
        out_specs=(VMEM,) * 5,
        name="second",
        compiler_params=params,
        cost_estimate=cost(40 * work),
    )(held, held_dout, early_out)
    relay_hop = relay
    relay, direct = lax.optimization_barrier((relay, direct))
    relay = lax.ppermute(relay, SECTION, far_pairs(count, half, [(2, last), (last - 2, 0)]))
    direct = lax.ppermute(direct, SECTION, far_pairs(count, half, [(0, last), (last, 0)]))
    kept = (held, early, late, values, out, inverse0, inverse1)
    grads, passed = pl.pallas_call(
        lambda *refs: near_kernel(half, *refs),
        out_shape=(three, whole),
        in_specs=[VMEM] * 8 + [ANY],
        out_specs=(HBM, VMEM),
        scratch_shapes=scratch,
        name="near",
        compiler_params=params,
        cost_estimate=cost(4 * work),
    )(*kept, near_dout, relay_hop)
    near_out = lax.ppermute(passed, SECTION, near_pairs(count, half, 1))
    token = pl.pallas_call(
        token_kernel,
        out_shape=jax.ShapeDtypeStruct((8, HD), jnp.float32),
        in_specs=[ANY] * 2,
        out_specs=VMEM,
        name="token",
        compiler_params=pltpu.CompilerParams(vmem_limit_bytes=2**20),
        cost_estimate=cost(40 * work),
    )(relay, direct)
    grads, attn_out = pl.pallas_call(
        lambda *refs: far_kernel(half, *refs),
        out_shape=(three, whole),
        in_specs=[HBM, ANY] + [VMEM] * 10,
        out_specs=(HBM, HBM),
        scratch_shapes=[*scratch, pltpu.SemaphoreType.DMA((2,))],
        input_output_aliases={0: 0},
        name="far",
        compiler_params=params,
        cost_estimate=cost(40 * work),
    )(grads, token, *kept, relay, direct, near_out)
    return (attn_out[None], grads.transpose(1, 0, 2)[None])


def solution(mesh):
    in_specs = (P("section", None, None, "tp"), P("section", None, "tp"))
    out_specs = (P("section", None, "tp"), P("section", None, None, "tp"))
    return jax.shard_map(
        on_device, mesh=mesh, in_specs=in_specs, out_specs=out_specs, check_vma=False
    )
```

```python
import math
import jax
import jax.numpy as jnp
from jax import lax
from jax.experimental import pallas as pl
from jax.experimental.pallas import tpu as pltpu
from jax.sharding import PartitionSpec as P

HD = 128
BLK = 256
SECTION = "section"
FACTOR = math.log2(math.e) / math.sqrt(HD)
SCALE = 1.0 / math.sqrt(HD)


def near_pairs(count, half, steps):
    pairs = [(source, (source + steps) % count) for source in range(count)]
    return [(source, target) for source, target in pairs if source // half == target // half]


def far_pairs(count, half, moves):
    return [
        (base + source, (base + half + target) % count)
        for base in range(0, count, half)
        for source, target in moves
    ]


def same_pairs(count, half, moves):
    return [(base + source, base + target) for base in range(0, count, half) for source, target in moves]


def dot_nt(a, b):
    return lax.dot_general(a, b, (((1,), (1,)), ((), ())), preferred_element_type=jnp.float32)


def dot_nn(a, b):
    return lax.dot_general(a, b, (((1,), (0,)), ((), ())), preferred_element_type=jnp.float32)


def dot_tn(a, b):
    return lax.dot_general(a, b, (((0,), (0,)), ((), ())), preferred_element_type=jnp.float32)


def lanes(head, wide=1):
    return slice(head * HD * wide, (head + 1) * HD * wide)


def attend(qkv_ref, values_ref, expo_ref, inverse_ref, out_ref, start, stop, base):
    q_at, k_at, own = slice(start, stop), slice(0, stop), slice(start - base, stop - base)
    for head in range(expo_ref.shape[0]):
        at = lanes(head)
        scores = dot_nt(qkv_ref[0, q_at, at], qkv_ref[1, k_at, at])
        rows = lax.broadcasted_iota(jnp.int32, scores.shape, 0) + start
        cols = lax.broadcasted_iota(jnp.int32, scores.shape, 1)
        scores = jnp.where(cols <= rows, scores, -jnp.inf)
        peak = jnp.max(scores, axis=1, keepdims=True)
        expo = jnp.exp2((scores - peak) * FACTOR).astype(jnp.bfloat16)
        expo_ref[head, own, k_at] = expo
        both = dot_nn(expo, values_ref[k_at, lanes(head, 2)])
        inverse = 1.0 / both[:, HD:]
        inverse_ref[own, at] = inverse
        out_ref[q_at, at] = (both[:, :HD] * inverse).astype(jnp.bfloat16)


def set_values(qkv_ref, values_ref, start, stop):
    for head in range(qkv_ref.shape[2] // HD):
        values_ref[start:stop, 2 * head * HD : (2 * head + 1) * HD] = qkv_ref[2, start:stop, lanes(head)]
        values_ref[start:stop, (2 * head + 1) * HD : (2 * head + 2) * HD] = jnp.ones((stop - start, HD), jnp.bfloat16)


def first_kernel(qkv_hbm, out_ref, expo_ref, inverse_ref, qkv_ref, values_ref, qkv_sem):
    cut = out_ref.shape[0]
    length = qkv_ref.shape[1]
    chunks = []
    for k, (start, stop) in enumerate(((0, BLK), (BLK, cut), (cut, length))):
        chunks.append(pltpu.make_async_copy(qkv_hbm.at[:, start:stop], qkv_ref.at[:, start:stop], qkv_sem.at[k]))
        chunks[k].start()
    for k, (start, stop) in enumerate(((0, BLK), (BLK, cut))):
        chunks[k].wait()
        set_values(qkv_ref, values_ref, start, stop)
        attend(qkv_ref, values_ref, expo_ref, inverse_ref, out_ref, start, stop, 0)
    rest = expo_ref.shape[2] - cut
    expo_ref[:, BLK:cut, cut:] = jnp.zeros((expo_ref.shape[0], cut - BLK, rest), jnp.bfloat16)
    chunks[2].wait()


def pick_kernel(half, out_ref, dout_ref, relay_ref, held_ref):
    sends_dout = lax.rem(lax.axis_index(SECTION), half) == 0
    held_ref[...] = dout_ref[...]

    @pl.when(sends_dout)
    def _():
        relay_ref[...] = dout_ref[0 : relay_ref.shape[0]]

    @pl.when(jnp.logical_not(sends_dout))
    def _():
        relay_ref[...] = out_ref[...]


def second_kernel(half, qkv_ref, dout_ref, early_ref, out_ref, direct_ref, expo_ref, inverse_ref, values_ref):
    length, width = out_ref.shape
    cut = early_ref.shape[0]
    set_values(qkv_ref, values_ref, 0, length)
    out_ref[0:cut] = early_ref[...]
    for start, stop in ((cut, 2 * BLK), (2 * BLK, length)):
        attend(qkv_ref, values_ref, expo_ref, inverse_ref, out_ref, start, stop, cut)
    sends_dout = lax.rem(lax.axis_index(SECTION), half) == 0

    @pl.when(sends_dout)
    def _():
        direct_ref[...] = dout_ref[cut:length]

    @pl.when(jnp.logical_not(sends_dout))
    def _():
        direct_ref[...] = out_ref[cut:length]


def gradients(refs, parts, grads_ref, dout_ref, stage_ref, scores_ref, sums_ref, grads_sem):
    qkv_ref, early_ref, late_ref, values_ref, out_ref = refs
    length, width = out_ref.shape
    heads = width // HD
    cut = early_ref.shape[1]
    copies = []

    def expo_of(head, start, stop, cols):
        pieces = []
        if start < cut:
            pieces.append(early_ref[head, start : min(stop, cut), cols])
        if stop > cut:
            pieces.append(late_ref[head, max(start, cut) - cut : stop - cut, cols])
        return pieces[0] if len(pieces) == 1 else jnp.concatenate(pieces, axis=0)

    def leave(which, head, at):
        copy = pltpu.make_async_copy(
            stage_ref.at[which, :, at], grads_ref.at[which, :, at], grads_sem.at[3 * head + which]
        )
        copy.start()
        return copy

    for head in range(heads):
        at, wide = lanes(head), lanes(head, 2)
        left = slice(2 * head * HD, (2 * head + 1) * HD)
        right = slice((2 * head + 1) * HD, (2 * head + 2) * HD)
        for start, stop, inverse_ref, ref in parts:
            scaled = ref[:, at].astype(jnp.float32) * inverse_ref[:, at]
            dout_ref[start:stop, left] = scaled.astype(jnp.bfloat16)
            product = scaled * out_ref[start:stop, at].astype(jnp.float32)
            dout_ref[start:stop, right] = (-product).astype(jnp.bfloat16)
        for first in range(0, length, BLK):
            k_at, q_at = slice(first, first + BLK), slice(first, length)
            grad_p = dot_nt(dout_ref[q_at, wide], values_ref[k_at, wide])
            expo = expo_of(head, first, length, k_at)
            grad_s = (expo.astype(jnp.float32) * grad_p).astype(jnp.bfloat16)
            scores_ref[q_at, k_at] = grad_s
            dq = dot_nn(grad_s, qkv_ref[1, k_at, at])
            sums_ref[0, q_at] = dq if first == 0 else sums_ref[0, q_at] + dq
        stage_ref[0, :, at] = (sums_ref[0] * SCALE).astype(jnp.bfloat16)
        copies.append(leave(0, head, at))
        for first in reversed(range(0, length, BLK)):
            q_at, k_at = slice(first, first + BLK), slice(0, first + BLK)
            dk = dot_tn(scores_ref[q_at, k_at], qkv_ref[0, q_at, at])
            dv = dot_tn(expo_of(head, first, first + BLK, k_at), dout_ref[q_at, left])
            last = first + BLK == length
            sums_ref[1, k_at] = dk if last else sums_ref[1, k_at] + dk
            sums_ref[2, k_at] = dv if last else sums_ref[2, k_at] + dv
        stage_ref[1, :, at] = (sums_ref[1] * SCALE).astype(jnp.bfloat16)
        copies.append(leave(1, head, at))
        stage_ref[2, :, at] = sums_ref[2].astype(jnp.bfloat16)
        copies.append(leave(2, head, at))

    for copy in copies:
        copy.wait()


def near_kernel(half, *refs):
    held, (first_ref, second_ref), (near_ref, _, grads_ref, passed_ref), work = refs[:5], refs[5:7], refs[7:11], refs[11:]
    cut, length = first_ref.shape[0], near_ref.shape[0]
    passed_ref[...] = held[4][...]

    @pl.when(lax.rem(lax.axis_index(SECTION), half) != half - 1)
    def _():
        parts = [(0, cut, first_ref, near_ref.at[0:cut]), (cut, length, second_ref, near_ref.at[cut:length])]
        gradients(held, parts, grads_ref, *work)


def token_kernel(*refs):
    refs[-1][...] = jnp.zeros_like(refs[-1])


def far_kernel(half, _, __, *refs):
    held, (first_ref, second_ref, relay_ref, direct_ref, near_ref, grads_ref, attn_ref), work = refs[:5], refs[5:12], refs[12:]
    work, sem = work[:-1], work[-1]
    cut, length = first_ref.shape[0], attn_ref.shape[0]
    place = lax.rem(lax.axis_index(SECTION), half)
    parts = [(0, cut, first_ref, relay_ref), (cut, length, second_ref, direct_ref)]

    def send(k, source):
        return pltpu.make_async_copy(source, attn_ref.at[parts[k][0] : parts[k][1]], sem.at[k])

    @pl.when(place == 0)
    def _():
        for k, part in enumerate(parts):
            send(k, part[3]).start()

    @pl.when(place != 0)
    def _():
        for k, part in enumerate(parts):
            send(k, near_ref.at[part[0] : part[1]]).start()

    @pl.when(place == half - 1)
    def _():
        gradients(held, parts, grads_ref, *work)

    for k, part in enumerate(parts):
        send(k, near_ref.at[part[0] : part[1]]).wait()


VMEM = pl.BlockSpec(memory_space=pltpu.VMEM)
HBM = pl.BlockSpec(memory_space=pltpu.HBM)
ANY = pl.BlockSpec(memory_space=pl.ANY)
FIRST_LIMIT = 49 * 2**20


def on_device(qkv_sent, grad_out):
    bf16 = jnp.bfloat16
    qkv = qkv_sent[0].transpose(1, 0, 2)
    dout = grad_out[0]
    _, length, width = qkv.shape
    heads = width // HD
    cut = length // 2
    count = lax.axis_size(SECTION)
    half = count // 2
    last = half - 1
    work = heads * length * length * HD
    whole = jax.ShapeDtypeStruct((length, width), bf16)
    part = jax.ShapeDtypeStruct((cut, width), bf16)
    three = jax.ShapeDtypeStruct(qkv.shape, bf16)
    inverse = jax.ShapeDtypeStruct((cut, width), jnp.float32)
    params = pltpu.CompilerParams(vmem_limit_bytes=24 * 2**20)
    scratch = [
        pltpu.VMEM((length, 2 * width), bf16),
        pltpu.VMEM(qkv.shape, bf16),
        pltpu.VMEM((length, length), bf16),
        pltpu.VMEM((3, length, HD), jnp.float32),
        pltpu.SemaphoreType.DMA((3 * heads,)),
    ]

    def cost(flops):
        return pl.CostEstimate(flops=flops, bytes_accessed=12 * length * width, transcendentals=0)

    early_out, early, inverse0, held = pl.pallas_call(
        first_kernel,
        out_shape=(part, jax.ShapeDtypeStruct((heads, cut, 2 * BLK), bf16), inverse, three),
        in_specs=[HBM],
        out_specs=(VMEM,) * 4,
        scratch_shapes=[pltpu.VMEM((cut, 2 * width), bf16), pltpu.SemaphoreType.DMA((3,))],
        name="first",
        compiler_params=pltpu.CompilerParams(vmem_limit_bytes=FIRST_LIMIT),
        cost_estimate=cost(work),
    )(qkv)
    relay, held_dout = pl.pallas_call(
        lambda *refs: pick_kernel(half, *refs),
        out_shape=(part, whole),
        in_specs=[VMEM] * 2,
        out_specs=(VMEM,) * 2,
        name="pick",
        compiler_params=pltpu.CompilerParams(vmem_limit_bytes=4 * 2**20),
        cost_estimate=cost(1),
    )(early_out, dout)
    relay = lax.ppermute(relay, SECTION, same_pairs(count, half, [(0, 2), (last, last - 2)]))
    near_dout = lax.ppermute(held_dout, SECTION, near_pairs(count, half, -1))
    out, direct, late, inverse1, values = pl.pallas_call(
        lambda *refs: second_kernel(half, *refs),
        out_shape=(
            whole,
            part,
            jax.ShapeDtypeStruct((heads, length - cut, length), bf16),
            inverse,
            jax.ShapeDtypeStruct((length, 2 * width), bf16),
        ),
        in_specs=[VMEM] * 3,
        out_specs=(VMEM,) * 5,
        name="second",
        compiler_params=params,
        cost_estimate=cost(40 * work),
    )(held, held_dout, early_out)
    relay_hop = relay
    relay, direct = lax.optimization_barrier((relay, direct))
    relay = lax.ppermute(relay, SECTION, far_pairs(count, half, [(2, last), (last - 2, 0)]))
    direct = lax.ppermute(direct, SECTION, far_pairs(count, half, [(0, last), (last, 0)]))
    kept = (held, early, late, values, out, inverse0, inverse1)
    grads, passed = pl.pallas_call(
        lambda *refs: near_kernel(half, *refs),
        out_shape=(three, whole),
        in_specs=[VMEM] * 8 + [ANY],
        out_specs=(HBM, VMEM),
        scratch_shapes=scratch,
        name="near",
        compiler_params=params,
        cost_estimate=cost(4 * work),
    )(*kept, near_dout, relay_hop)
    near_out = lax.ppermute(passed, SECTION, near_pairs(count, half, 1))
    token = pl.pallas_call(
        token_kernel,
        out_shape=jax.ShapeDtypeStruct((8, HD), jnp.float32),
        in_specs=[ANY] * 2,
        out_specs=VMEM,
        name="token",
        compiler_params=pltpu.CompilerParams(vmem_limit_bytes=2**20),
        cost_estimate=cost(40 * work),
    )(relay, direct)
    grads, attn_out = pl.pallas_call(
        lambda *refs: far_kernel(half, *refs),
        out_shape=(three, whole),
        in_specs=[HBM, ANY] + [VMEM] * 10,
        out_specs=(HBM, HBM),
        scratch_shapes=[*scratch, pltpu.SemaphoreType.DMA((2,))],
        input_output_aliases={0: 0},
        name="far",
        compiler_params=params,
        cost_estimate=cost(40 * work),
    )(grads, token, *kept, relay, direct, near_out)
    return (attn_out[None], grads.transpose(1, 0, 2)[None])


def solution(mesh):
    in_specs = (P("section", None, None, "tp"), P("section", None, "tp"))
    out_specs = (P("section", None, "tp"), P("section", None, None, "tp"))
    return jax.shard_map(
        on_device, mesh=mesh, in_specs=in_specs, out_specs=out_specs, check_vma=False
    )
```
